32 devices in a mesh: azim: 8 (over y, x, core), axial: 4 (over z).
Axes of the slice: x: 2, y: 2, z: 4, core: 2. Of those that a mesh axis runs over, the one named last changes fastest.
Arguments:
- fraction: float32 [2048, 64, 512], P('azim', 'axial'), may hold values from 0 to 1
- normals: bfloat16 [3, 2048, 64, 512], P(None, 'azim', 'axial'), may hold values from -0.63 to 0.63, as said below
- planes: bfloat16 [2048, 64, 512], P('azim', 'axial'), may hold values from 0 to 1
- cell_flags: int32 [2048, 64, 512], P('azim', 'axial'), may hold values from 0 to 2
- courant: bfloat16 [3, 2048, 64, 512], P(None, 'azim', 'axial'), may hold values from -0.29882812 to 0.29882812
- radial_basis: float32 [512, 512], replicated, may hold values from -0.25 to 0.25
- axial_basis: float32 [64, 64], replicated, may hold values from -0.75 to 0.75
- radial_rates: float32 [512], replicated, may hold values from 0.5 to 4
- axial_rates: float32 [64], replicated, may hold values from 0.2 to 2
Outputs:
- fraction_new: float32 [2048, 64, 512], P('azim', 'axial')
- pressure: float32 [2048, 64, 512], P('azim', 'axial')
The draws below stay inside these ranges and needn't reach their ends.
Inputs may be any that keep to these rules, and one draw needn't show every extreme that they name: `normals`: every component's magnitude is 0.12 or more, and a cell's three magnitudes sum to 1 within bfloat16 rounding.
All inputs are finite; a program needn't handle non-finite values.
Results may differ from the reference program's by a relative error of at most 0.0003.
Values may be sent and summed in bfloat16 or wider, within the bound.
A program may use at most 256 MiB of HBM per device.

```python
import math
import jax
import jax.numpy as jnp
from jax import lax

R = 512
A = 2048
Z = 64


def draw_normals(key, part):
    first_key, second_key = jax.random.split(key)
    uniforms = jax.random.uniform(first_key, (3, A, Z, R), jnp.float32)
    magnitudes = 0.4 + 0.6 * uniforms
    signs = jnp.where(jax.random.bernoulli(second_key, 0.5, (3, A, Z, R)), 1.0, -1.0)
    totals = magnitudes[0] + magnitudes[1] + magnitudes[2]
    return (signs * magnitudes / totals[None]).astype(jnp.bfloat16)


def plant(values, stream_key, least, top_value):
    longest = values.shape.index(max(values.shape))
    spots = []
    for shift in (0, 1):
        where = [jax.random.randint(jax.random.fold_in(stream_key, axis), (), 0, length) for axis, length in enumerate(values.shape)]
        where[longest] = (where[longest] + shift) % values.shape[longest]
        spots.append(tuple(where))
    return values.at[spots[0]].set(least).at[spots[1]].set(top_value)


def block_scale(key, shape, shards, low, largest):
    loudness = 1.0
    for dim, shards_of in shards:
        heights = jax.random.uniform(jax.random.fold_in(jax.random.fold_in(key, 6), dim), (shards_of,), jnp.float32, low / len(shards), largest / len(shards))
        loudness = loudness * jnp.repeat(jnp.exp(heights), shape[dim] // shards_of).reshape((-1,) + (1,) * (len(shape) - 1 - dim))
    return loudness


def normal_values(own_key, dims, spread, most, held_as=jnp.bfloat16):
    values = jax.random.normal(own_key, dims, jnp.float32) * spread
    return jnp.minimum(jnp.maximum(values, -most), most).astype(held_as)


def setup_inputs(seed: int = 0) -> dict:
    arg_keys = jax.random.split(jax.random.key(seed), 10)
    fraction = jnp.clip(1.0 * jax.random.uniform(arg_keys[0], (A, Z, R), jnp.float32) ** block_scale(arg_keys[0], (A, Z, R), ((0, 8), (1, 4)), -0.2, 0.2), 0.0, 1.0)
    normals = draw_normals(jax.random.fold_in(arg_keys[9], 71), 0)
    planes = jnp.clip(1.0 * jax.random.uniform(arg_keys[2], (A, Z, R), jnp.float32) ** block_scale(arg_keys[2], (A, Z, R), ((0, 8), (1, 4)), -0.2, 0.2), 0.0, 1.0).astype(jnp.bfloat16)
    cell_flags = plant(jax.random.randint(arg_keys[3], (A, Z, R), 0, 3), jax.random.fold_in(arg_keys[3], 1), 0, 2).astype(jnp.int32)
    courant = jnp.clip(jax.random.uniform(arg_keys[4], (3, A, Z, R), jnp.float32, -0.29882812, 0.29882812) * block_scale(arg_keys[4], (3, A, Z, R), ((1, 8), (2, 4)), -0.4, 0.0), -0.29882812, 0.29882812).astype(jnp.bfloat16)
    radial_basis = normal_values(arg_keys[5], (R, R), R ** -0.5, 0.25, jnp.float32)
    axial_basis = normal_values(arg_keys[6], (Z, Z), Z ** -0.5, 0.75, jnp.float32)
    radial_rates = jnp.clip(jnp.exp(jax.random.uniform(arg_keys[7], (R,), jnp.float32, math.log(0.5), math.log(4.0))), 0.5, 4.0)
    axial_rates = jnp.clip(jnp.exp(jax.random.uniform(arg_keys[8], (Z,), jnp.float32, math.log(0.2), math.log(2.0))), 0.2, 2.0)
    return dict(fraction=fraction, normals=normals, planes=planes, cell_flags=cell_flags, courant=courant, radial_basis=radial_basis, axial_basis=axial_basis, radial_rates=radial_rates, axial_rates=axial_rates)


HIGHEST = lax.Precision.HIGHEST
BUOYANCY = 0.5


def cut_volume(magnitudes, alpha_value, direction, lower_end, thickness):
    offset = alpha_value - magnitudes[direction] * lower_end
    summed = jnp.zeros_like(offset)
    for corner in range(8):
        height = offset
        parity = 1.0
        for coord_axis in range(3):
            if (corner >> coord_axis) & 1:
                parity = -parity
                if coord_axis == direction:
                    height = height - magnitudes[coord_axis] * thickness
                else:
                    height = height - magnitudes[coord_axis]
        summed = summed + parity * jnp.maximum(height, 0.0) ** 3
    return summed / (6.0 * magnitudes[0] * magnitudes[1] * magnitudes[2])


def slab_volume(cell, direction, upper_side, thickness):
    normal, alpha_value, flag_value = cell
    components = [normal[component].astype(jnp.float32) for component in range(3)]
    magnitudes = [jnp.abs(component_value) for component_value in components]
    negative = components[direction] < 0.0
    if upper_side:
        lower_end = jnp.where(negative, 0.0, 1.0 - thickness)
    else:
        lower_end = jnp.where(negative, 1.0 - thickness, 0.0)
    mixed = cut_volume(magnitudes, alpha_value.astype(jnp.float32), direction, lower_end, thickness)
    return jnp.where(flag_value == 1, thickness, jnp.where(flag_value == 2, mixed, 0.0))


def donor_flux(lower_cell, upper_cell, face_speed, direction, lower_weight, upper_weight):
    forward = jnp.maximum(face_speed, 0.0)
    backward = jnp.maximum(-face_speed, 0.0)
    from_lower = slab_volume(lower_cell, direction, True, forward) * lower_weight
    from_upper = slab_volume(upper_cell, direction, False, backward) * upper_weight
    return jnp.where(face_speed > 0.0, from_lower, jnp.where(face_speed < 0.0, -from_upper, 0.0))


def roll_next(field, direction):
    return jnp.roll(field, -1, axis=direction + field.ndim - 3)


def reference(fraction, normals, planes, cell_flags, courant, radial_basis, axial_basis, radial_rates, axial_rates):
    velocity = courant.astype(jnp.float32)
    radius = 1.0 + (jnp.arange(R, dtype=jnp.float32) + 0.5) / R
    face_radius = 1.0 + (jnp.arange(R - 1, dtype=jnp.float32) + 1.0) / R
    cell = (normals, planes, cell_flags)
    updated = fraction
    divergence = jnp.zeros_like(fraction)
    for direction in range(2):
        upper_cell = (roll_next(normals, direction), roll_next(planes, direction), roll_next(cell_flags, direction))
        face_speed = 0.5 * (velocity[direction] + roll_next(velocity[direction], direction))
        face_flux = donor_flux(cell, upper_cell, face_speed, direction, 1.0, 1.0)
        updated = updated - (face_flux - jnp.roll(face_flux, 1, axis=direction))
        divergence = divergence + (face_speed - jnp.roll(face_speed, 1, axis=direction))
    lower_cell = (normals[..., :-1], planes[..., :-1], cell_flags[..., :-1])
    upper_cell = (normals[..., 1:], planes[..., 1:], cell_flags[..., 1:])
    face_speed = 0.5 * (velocity[2][..., :-1] + velocity[2][..., 1:])
    face_flux = donor_flux(lower_cell, upper_cell, face_speed, 2, radius[:-1], radius[1:])
    zeros_col = jnp.zeros_like(fraction[..., :1])
    upper_flux = jnp.concatenate([face_flux, zeros_col], axis=-1)
    lower_flux = jnp.concatenate([zeros_col, face_flux], axis=-1)
    updated = updated - (upper_flux - lower_flux) / radius
    face_moved = face_radius * face_speed
    divergence = divergence + (jnp.concatenate([face_moved, zeros_col], axis=-1) - jnp.concatenate([zeros_col, face_moved], axis=-1)) / radius
    source = divergence + BUOYANCY * updated
    radial_modes = jnp.einsum('azr,rj->azj', source, radial_basis, precision=HIGHEST)
    both_modes = jnp.einsum('azj,zn->anj', radial_modes, axial_basis, precision=HIGHEST)
    spectrum = jnp.fft.rfft(both_modes, axis=0)
    half_count = A // 2
    coefficients = jnp.concatenate([spectrum.real, -spectrum.imag[1:half_count]], axis=0)
    mode_index = jnp.arange(A)
    wavenumber = jnp.where(mode_index <= half_count, mode_index, mode_index - half_count).astype(jnp.float32)
    azim_rates = 2.0 - 2.0 * jnp.cos(2.0 * jnp.pi * wavenumber / A)
    denominator = azim_rates[:, None, None] + axial_rates[None, :, None] + radial_rates[None, None, :]
    solved = coefficients / denominator
    cosines = solved[: half_count + 1]
    sines = jnp.concatenate([jnp.zeros_like(solved[:1]), solved[half_count + 1:], jnp.zeros_like(solved[:1])], axis=0)
    physical = jnp.fft.irfft(cosines - 1j * sines, n=A, axis=0)
    physical = jnp.einsum('anj,zn->azj', physical, axial_basis, precision=HIGHEST)
    pressure = jnp.einsum('azj,rj->azr', physical, radial_basis, precision=HIGHEST)
    return updated, pressure
```

```python
import functools

import jax
import jax.numpy as jnp
import numpy as np
from jax import lax
from jax.experimental import pallas as pl
from jax.experimental.pallas import tpu as pltpu
from jax.sharding import PartitionSpec as P

HIGH = lax.Precision.HIGH
BUOYANCY = 0.5
CODE_TOP = 32700.0


def shifted_in(edge, axis, towards_lower):
    count = lax.axis_size(axis)
    if towards_lower:
        pairs = [((i + 1) % count, i) for i in range(count)]
    else:
        pairs = [(i, (i + 1) % count) for i in range(count)]
    return lax.ppermute(edge, axis, pairs)


def cell_parts(n0, n1, n2, code):
    m0, m1, m2 = jnp.abs(n0), jnp.abs(n1), jnp.abs(n2)
    return (n0, n1, n2, code, 1.0 / (6.0 * m0 * m1 * m2))


def cube(height):
    held = jnp.maximum(height, 0.0)
    return held * held * held


def face_flux(direction, lower, upper, speed, lower_weight=None, upper_weight=None):
    forward = speed > 0.0
    signed = jnp.where(forward, lower[direction], -upper[direction])
    first, second = [d for d in range(3) if d != direction]
    along = jnp.abs(signed)
    side_a = jnp.abs(jnp.where(forward, lower[first], upper[first]))
    side_b = jnp.abs(jnp.where(forward, lower[second], upper[second]))
    code = jnp.where(forward, lower[3], upper[3])
    inverse = jnp.where(forward, lower[4], upper[4])
    width = jnp.abs(speed)
    near = code - along * jnp.where(signed < 0.0, 0.0, 1.0 - width)
    far = near - along * width
    sides = side_a + side_b
    total = (cube(near) - cube(near - side_a)) - (cube(near - side_b) - cube(near - sides))
    total = total - ((cube(far) - cube(far - side_a)) - (cube(far - side_b) - cube(far - sides)))
    volume = jnp.where(code > 3.0, width, jnp.where(code < -0.5, 0.0, total * inverse))
    if lower_weight is not None:
        volume = volume * jnp.where(forward, lower_weight, upper_weight)
    return jnp.where(forward, volume, jnp.where(speed < 0.0, -volume, 0.0))


def advect_kernel(
    fraction_ref,
    normals_ref,
    planes_ref,
    flags_ref,
    courant_ref,
    next_ref,
    high_ref,
    low_azim_ref,
    low_axial_ref,
    updated_ref,
    source_ref,
    kept,
):
    rows, layers, cells = fraction_ref.shape
    f32 = jnp.float32

    @pl.when(pl.program_id(0) == 0)
    def _():
        kept[...] = low_azim_ref[...]

    index = lax.broadcasted_iota(jnp.int32, (1, cells), 1)
    place = index.astype(f32)
    radius = 1.0 + (place + 0.5) / cells
    next_radius = 1.0 + (place + 1.5) / cells
    face_radius = 1.0 + (place + 1.0) / cells
    inverse_radius = 1.0 / radius
    inner = lax.broadcasted_iota(jnp.int32, (layers, cells), 1) < cells - 1
    layer = lax.broadcasted_iota(jnp.int32, (layers, cells), 0)
    last_layer = layer == layers - 1
    first_layer = layer == 0

    def row_parts(row):
        flags = flags_ref[row]
        code = jnp.where(
            flags == 2, planes_ref[row].astype(f32), jnp.where(flags == 1, 4.0, -1.0)
        )
        return cell_parts(
            normals_ref[0, row].astype(f32),
            normals_ref[1, row].astype(f32),
            normals_ref[2, row].astype(f32),
            code,
        )

    def one_row(row, upper, upper_speed):
        own = row_parts(row)
        moved = [courant_ref[d, row].astype(f32) for d in range(3)]
        speed = 0.5 * (moved[0] + upper_speed)
        flux = face_flux(0, own, upper, speed)
        gained = flux - kept[0]
        divergence = speed - kept[1]
        kept[0] = flux
        kept[1] = speed
        beyond = cell_parts(*[high_ref[k, row] for k in range(4)])
        above = [
            jnp.where(last_layer, high, pltpu.roll(field, layers - 1, 0))
            for field, high in zip(own, beyond)
        ]
        speed = 0.5 * (
            moved[1]
            + jnp.where(last_layer, high_ref[4, row], pltpu.roll(moved[1], layers - 1, 0))
        )
        flux = face_flux(1, own, above, speed)
        gained = gained + (
            flux - jnp.where(first_layer, low_axial_ref[0, row], pltpu.roll(flux, 1, 0))
        )
        divergence = divergence + (
            speed - jnp.where(first_layer, low_axial_ref[1, row], pltpu.roll(speed, 1, 0))
        )
        outer = [pltpu.roll(field, cells - 1, 1) for field in own]
        speed = 0.5 * (moved[2] + pltpu.roll(moved[2], cells - 1, 1))
        speed = jnp.where(inner, speed, 0.0)
        flux = face_flux(2, own, outer, speed, radius, next_radius)
        gained = gained + (flux - pltpu.roll(flux, 1, 1)) * inverse_radius
        carried = face_radius * speed
        divergence = divergence + (carried - pltpu.roll(carried, 1, 1)) * inverse_radius
        updated = fraction_ref[row] - gained
        updated_ref[row] = updated
        source_ref[row] = divergence + BUOYANCY * updated

    def step(row, _):
        one_row(row, row_parts(row + 1), courant_ref[0, row + 1].astype(f32))
        return 0

    lax.fori_loop(0, rows - 1, step, 0)
    one_row(
        rows - 1,
        cell_parts(*[next_ref[k, 0].astype(f32) for k in range(4)]),
        next_ref[4, 0].astype(f32),
    )


def plane_codes(planes, flags):
    return jnp.where(
        flags == 2, planes.astype(jnp.float32), jnp.where(flags == 1, 4.0, -1.0)
    ).astype(jnp.bfloat16)


def packed_edge(normals, planes, flags, courant, direction, pick):
    parts = [pick(normals[d]) for d in range(3)]
    parts.append(plane_codes(pick(planes), pick(flags)))
    parts.append(pick(courant[direction]))
    return jnp.stack(parts)


def low_face(direction, lower, upper):
    lower, upper = lower.astype(jnp.float32), upper.astype(jnp.float32)
    speed = 0.5 * (lower[4] + upper[4])
    flux = face_flux(direction, cell_parts(*lower[:4]), cell_parts(*upper[:4]), speed)
    return jnp.stack([flux, speed])


def advect(fraction, normals, planes, flags, courant):
    rows, layers, cells = fraction.shape
    block = 16 if rows % 16 == 0 else 1
    blocks = rows // block
    fields = (normals, planes, flags, courant)
    top_row = packed_edge(*fields, 0, lambda x: x[rows - 1])
    bottom_row = packed_edge(*fields, 0, lambda x: x[0])
    top_layer = packed_edge(*fields, 1, lambda x: x[:, layers - 1])
    bottom_layer = packed_edge(*fields, 1, lambda x: x[:, 0])
    high_row = shifted_in(bottom_row, "azim", True)
    low_row = shifted_in(top_row, "azim", False)
    high_layer = shifted_in(bottom_layer, "axial", True)
    low_layer = shifted_in(top_layer, "axial", False)
    low_azim = low_face(0, low_row, bottom_row)
    low_axial = low_face(1, low_layer, bottom_layer)[:, :, None]
    high_axial = high_layer.astype(jnp.float32)[:, :, None]
    inside = packed_edge(*fields, 0, lambda x: x[block::block])
    following = jnp.concatenate([inside, high_row[:, None]], axis=1)
    whole = pl.BlockSpec((block, layers, cells), lambda i: (i, 0, 0))
    triple = pl.BlockSpec((3, block, layers, cells), lambda i: (0, i, 0, 0))
    return pl.pallas_call(
        advect_kernel,
        grid=(blocks,),
        in_specs=[
            whole,
            triple,
            whole,
            whole,
            triple,
            pl.BlockSpec((5, 1, layers, cells), lambda i: (0, i, 0, 0)),
            pl.BlockSpec((5, block, 1, cells), lambda i: (0, i, 0, 0)),
            pl.BlockSpec((2, layers, cells), lambda i: (0, 0, 0)),
            pl.BlockSpec((2, block, 1, cells), lambda i: (0, i, 0, 0)),
        ],
        out_specs=[whole, whole],
        out_shape=[jax.ShapeDtypeStruct(fraction.shape, jnp.float32)] * 2,
        scratch_shapes=[pltpu.VMEM((2, layers, cells), jnp.float32)],
        compiler_params=pltpu.CompilerParams(vmem_limit_bytes=40 * 2**20),
    )(
        fraction,
        normals,
        planes,
        flags,
        courant,
        following,
        high_axial,
        low_azim,
        low_axial,
    )


def coded(values):
    most = jnp.max(jnp.abs(values), axis=-1)
    exponent = jnp.clip(jnp.ceil(jnp.log2(most) * 256.0) + 1.0, -30000.0, 30000.0)
    scale = CODE_TOP * jnp.exp2(exponent * (-1.0 / 256.0))
    codes = jnp.round(values * scale[..., None])
    return jnp.clip(codes, -32767.0, 32767.0).astype(jnp.int16), exponent.astype(jnp.int16)


def exchange(values):
    modes, cells = values.shape[1], values.shape[3]
    codes, exponent = coded(values)
    extra = jnp.pad(exponent.transpose(0, 2, 1), ((0, 0), (0, 0), (0, cells - modes)))
    sent = jnp.concatenate([codes, extra[:, None]], axis=1)
    got = lax.all_to_all(sent, ("azim", "axial"), split_axis=0, concat_axis=0, tiled=True)
    exponent = got[:, modes, :, :modes].transpose(0, 2, 1).astype(jnp.float32)
    scale = jnp.exp2(exponent * (1.0 / 256.0)) * (1.0 / CODE_TOP)
    return got[:, :modes].astype(jnp.float32) * scale[..., None]


@functools.lru_cache(None)
def azimuth_tables(total):
    half, quarter = total // 2, total // 4
    place = np.arange(half)

    def table(cosines, sines):
        waves = np.concatenate([cosines, sines])
        angles = 2.0 * np.pi / total * (waves[:, None] * place[None, :] % total)
        rows = np.concatenate(
            [np.cos(angles[: len(cosines)]), np.sin(angles[len(cosines) :])]
        ).astype(np.float32)
        rates = (2.0 - 2.0 * np.cos(2.0 * np.pi * waves / total)).astype(np.float32)
        ends = (waves == 0) | (waves == half)
        return rows, rates, (np.where(ends, 1.0, 2.0) / total).astype(np.float32)

    even = 2 * np.arange(quarter + 1)
    odd = 2 * np.arange(quarter) + 1
    return table(even, even[1:-1]), table(odd, odd)


def local(
    fraction,
    normals,
    planes,
    cell_flags,
    courant,
    radial_basis,
    axial_basis,
    radial_rates,
    axial_rates,
):
    rows, layers, cells = fraction.shape
    around, along = lax.axis_size("azim"), lax.axis_size("axial")
    devices = around * along
    modes = cells // devices
    total = rows * around
    half = total // 2
    updated, source = advect(fraction, normals, planes, cell_flags, courant)
    radial_modes = jnp.einsum("azr,rj->jza", source, radial_basis, precision=HIGH)
    got = exchange(radial_modes.reshape(devices, modes, layers, rows))
    got = got.reshape(around, along, modes, layers, rows).transpose(2, 1, 3, 0, 4)
    got = got.reshape(modes, along * layers, total)
    both = jnp.einsum("jza,zn->jna", got, axial_basis, precision=HIGH)
    first = (lax.axis_index("azim") * along + lax.axis_index("axial")) * modes
    shifts = lax.dynamic_slice_in_dim(radial_rates, first, modes)[:, None] + axial_rates[None, :]
    low, high = both[..., :half], both[..., half:]
    solved = []
    for folded, (table, rates, weight) in zip((low + high, low - high), azimuth_tables(total)):
        coefficients = jnp.einsum("jna,ka->jnk", folded, table, precision=HIGH)
        scaled = coefficients / (rates + shifts[..., None]) * weight
        solved.append(jnp.einsum("jnk,ka->jna", scaled, table, precision=HIGH))
    physical = jnp.concatenate([solved[0] + solved[1], solved[0] - solved[1]], axis=-1)
    physical = jnp.einsum("jna,zn->jza", physical, axial_basis, precision=HIGH)
    physical = physical.reshape(modes, along, layers, around, rows).transpose(3, 1, 0, 2, 4)
    returned = exchange(physical.reshape(devices, modes, layers, rows))
    returned = returned.reshape(cells, layers, rows)
    pressure = jnp.einsum("jza,rj->azr", returned, radial_basis, precision=HIGH)
    return (updated, pressure)


def solution(mesh):
    placed = (
        P("azim", "axial", None),
        P(None, "azim", "axial", None),
        P("azim", "axial", None),
        P("azim", "axial", None),
        P(None, "azim", "axial", None),
        P(),
        P(),
        P(),
        P(),
    )
    return jax.shard_map(
        local,
        mesh=mesh,
        in_specs=placed,
        out_specs=(P("azim", "axial", None), P("azim", "axial", None)),
        check_vma=False,
    )
```
